32 devices in a mesh: groups: 2 (over y), blk: 4 (over z), proj: 2 (over x), rep: 2 (over core).
Axes of the slice: x: 2, y: 2, z: 4, core: 2. Of those that a mesh axis runs over, the one named last changes fastest.
Arguments:
- activations: bfloat16 [36864, 4096], P(('groups', 'blk', 'rep'), 'proj'), parts along dimension 0, may hold values from -6 to 6
- out_grads: bfloat16 [36864, 4096], P(('groups', 'blk', 'rep'), 'proj'), parts along dimension 0, may hold values from -6 to 6
- in_proj: bfloat16 [4096, 64], P('proj'), may hold values from -0.09375 to 0.09375
- out_proj: bfloat16 [4096, 64], P('proj'), may hold values from -0.09375 to 0.09375
- precond_queries: bfloat16 [128, 4096], P(('blk', 'rep'), 'proj'), may hold values from -0.03125 to 0.03125
- counts: int32 [16, 256], P(('groups', 'blk', 'rep')), parts along dimension 0, may hold values from 1 to 576, 2304 in all within a row
- owners: int32 [16, 256], P(('groups', 'blk', 'rep')), parts along dimension 0, may hold values from 0 to 3, as said below
Outputs:
- scores: float32 [128, 4096], P('proj', ('groups', 'blk', 'rep')), parts along dimension 1
The draws below stay inside these ranges and needn't reach their ends.
There are 2 independent parts, one for each index of `groups`. The reference program is written for one: setup_inputs(seed, part) draws one part's arguments, and reference() takes and returns one part's arrays. A program takes and returns all parts, laid end to end along the dimension named above; an argument that names none is the same for every part. Nothing has to cross between parts.
Inputs may be any that keep to these rules, and one draw needn't show every extreme that they name: Each row lists the counts of one shard's documents in order; a row sums to 2304, and its largest count is 576. `owners`: no owner is named by more than 64 documents of one shard; one owner is named by exactly 64 documents of every shard.
All inputs are finite; a program needn't handle non-finite values.
Results may differ from the reference program's by a relative error of at most 0.0041.
Values may be sent and summed in bfloat16 or wider, within the bound.
A program may use at most 128 MiB of HBM per device.

```python
import math
import jax
import jax.numpy as jnp
import numpy as np
from jax import lax

DIN = 4096
DOUT = 4096
KI = 64
KO = 64
TOK_SH = 2304
DOC_SH = 256
DOC_MOST = 576
FEAT = 4096
CAP = 64
OWNERS = 4
REPS = 2
SHARDS = 8
TOKENS = 18432
DOCS = 2048
QUERIES = 128
SLOTS = 2048


def draw_owners(key, part):
    key = jax.random.fold_in(key, 7)
    hot_key, row_key = jax.random.split(key)
    hot_owner = jax.random.randint(hot_key, (), 0, OWNERS).astype(jnp.int32)

    def one_row(shard_key):
        order_key, slot_key = jax.random.split(shard_key)
        order = jax.random.permutation(order_key, DOC_SH).astype(jnp.int32)
        picked = jax.random.permutation(slot_key, (OWNERS - 1) * CAP).astype(jnp.int32)[:DOC_SH - CAP]
        others = picked // CAP
        others = others + (others >= hot_owner).astype(jnp.int32)
        sequence = jnp.concatenate([jnp.full((CAP,), 1, jnp.int32) * hot_owner, others])
        inverse = jnp.argsort(order)
        return sequence[inverse].astype(jnp.int32)
    return jax.vmap(one_row)(jax.random.split(row_key, SHARDS))


def block_levels(stream_key, extent, cuts, least, top_value):
    def one(dim, shards_of):
        steps = jax.random.uniform(jax.random.fold_in(jax.random.fold_in(stream_key, 6), dim), (shards_of,), jnp.float32, least / len(cuts), top_value / len(cuts))
        return jnp.repeat(jnp.exp(steps), extent[dim] // shards_of).reshape((-1,) + (1,) * (len(extent) - dim - 1))

    gain = one(*cuts[0])
    for cut in cuts[1:]:
        gain = gain * one(*cut)
    return gain


def profile(amount, total, most, skew):
    portions = [(1 << 20) // math.isqrt(rank ** skew) + 1 for rank in range(2, amount + 1)]
    surplus, given = total - most - (amount - 1), [1] * (amount - 1)
    while surplus > 0:
        movable = [i for i in range(amount - 1) if given[i] < most]
        mass, left = sum([portions[i] for i in movable]), surplus
        for i in movable:
            extra = min(most - given[i], max(1, left * portions[i] // mass), surplus)
            given[i] = given[i] + extra
            surplus = surplus - extra
    return np.array([most] + given)


def uneven_parts(rng, number_of, total, limit, skew):
    if number_of == 2:
        one = jax.random.randint(rng, (), max(1, total - limit), min(limit, total - 1) + 1)
        return jnp.stack([one, total - one])
    tallies = jnp.asarray(profile(number_of, total, limit, skew), jnp.int32)
    pairs = (number_of - 1) // 2
    source_of, taker = tallies[1:1 + 2 * pairs:2], tallies[2:2 + 2 * pairs:2]
    slack = jnp.minimum(source_of - 1, limit - taker)
    moved = jax.random.randint(jax.random.fold_in(rng, 1), (pairs,), 0, 1 << 20) % (slack + 1)
    tallies = tallies.at[1:1 + 2 * pairs:2].set(source_of - moved).at[2:2 + 2 * pairs:2].set(taker + moved)
    return tallies[jax.random.permutation(jax.random.fold_in(rng, 2), number_of)]


def scatter_about(own_key, extent, spread, bound, shards=(), kind=jnp.bfloat16):
    drawn = spread * jax.random.normal(own_key, extent, jnp.float32)
    if shards:
        drawn = drawn * block_levels(own_key, extent, shards, -0.22, 0.18)
    return jnp.clip(drawn, -bound, bound).astype(kind)


def setup_inputs(seed: int = 0, part: int = 0) -> dict:
    splits = jax.random.split(jax.random.key(seed), 8)
    part_keys = jax.random.split(jax.random.fold_in(splits[7], part), 8)
    return {
        "activations": scatter_about(part_keys[0], (TOKENS, DIN), 1.0, 6.0, ((0, 8), (1, 2))),
        "out_grads": scatter_about(part_keys[1], (TOKENS, DOUT), 1.0, 6.0, ((0, 8), (1, 2))),
        "in_proj": scatter_about(splits[2], (DIN, KI), DIN ** -0.5, 0.09375, ((0, 2),)),
        "out_proj": scatter_about(splits[3], (DOUT, KO), DOUT ** -0.5, 0.09375, ((0, 2),)),
        "precond_queries": scatter_about(splits[4], (QUERIES, FEAT), (8 * FEAT) ** -0.5, 0.03125, ((0, 8), (1, 2))),
        "counts": jax.vmap(lambda own: uneven_parts(own, DOC_SH, TOK_SH, DOC_MOST, 2))(jax.random.split(part_keys[5], SHARDS)).reshape((SHARDS, DOC_SH)).astype(jnp.int32),
        "owners": draw_owners(jax.random.fold_in(jax.random.fold_in(splits[7], part), 71), part),
    }


def shard_grads(inputs):
    in_rows, out_rows, lengths = inputs
    token_grads = (in_rows[:, :, None] * out_rows[:, None, :]).reshape(TOK_SH, KI * KO).astype(jnp.bfloat16)
    doc_ends = jnp.cumsum(lengths).astype(jnp.int32)
    position = jnp.arange(TOK_SH, dtype=jnp.int32)
    doc_ids = jnp.sum((doc_ends[None, :] <= position[:, None]).astype(jnp.int32), axis=1)
    summed = jax.ops.segment_sum(token_grads.astype(jnp.float32), doc_ids, num_segments=DOC_SH)
    return summed.astype(jnp.bfloat16)


def reference(activations, out_grads, in_proj, out_proj, precond_queries, counts, owners):
    in_factor = jnp.dot(activations, in_proj, preferred_element_type=jnp.float32)
    out_factor = jnp.dot(out_grads, out_proj, preferred_element_type=jnp.float32)
    doc_grads = lax.map(shard_grads, (in_factor.reshape(SHARDS, TOK_SH, KI), out_factor.reshape(SHARDS, TOK_SH, KO), counts))
    doc_grads = doc_grads.reshape(DOCS, FEAT)
    doc_scores = jnp.dot(precond_queries, doc_grads.T, preferred_element_type=jnp.float32)
    onehot = (owners[:, :, None] == jnp.arange(OWNERS, dtype=jnp.int32)[None, None, :]).astype(jnp.int32)
    earlier = jnp.cumsum(onehot, axis=1).astype(jnp.int32) - onehot
    slot_rank = jnp.sum(earlier * onehot, axis=2).astype(jnp.int32)
    shard_index = jnp.arange(SHARDS, dtype=jnp.int32)[:, None]
    sender = shard_index // REPS
    copy_index = shard_index % REPS
    column = ((owners * REPS + copy_index) * OWNERS + sender) * CAP + slot_rank
    scores = jnp.zeros((QUERIES, SLOTS), jnp.float32).at[:, column.reshape(-1)].set(doc_scores)
    return scores
```

```python
import functools

import jax
import jax.numpy as jnp
from jax import lax
from jax.experimental import pallas as pl
from jax.experimental.pallas import tpu as pltpu
from jax.sharding import PartitionSpec as P

CAP = 64
F32 = jnp.float32
BF16 = jnp.bfloat16


def kernel(sizes, act, og, wi, wo, qin, counts, owners, out, abuf, gbuf, wraw, wpad, qbuf, sbuf,
           rbuf, dg, dgb, ft, scores, spack, rpack, load_a, load_g, load_w, load_q, fsend, frecv,
           a_send, a_recv, b_send, b_recv, c_send, c_recv, d_send, d_recv, s_send, s_recv):
    ny, nz, nx, nc, part, chunk = sizes
    steps = part // chunk
    x, y = lax.axis_index("proj"), lax.axis_index("groups")
    z, c = lax.axis_index("blk"), lax.axis_index("rep")
    ki, ko = wi.shape[1], wo.shape[1]
    width = qbuf.shape[-1]
    qrows = qin.shape[0]
    docs = counts.shape[1]
    columns = nz * CAP

    def put(src, dst, send, recv, **where):
        return pltpu.make_async_remote_copy(
            src_ref=src, dst_ref=dst, send_sem=send, recv_sem=recv,
            device_id=where, device_id_type=pl.DeviceIdType.MESH,
        )

    def at(index, step, n):
        return lax.rem(index + step, n)

    w_loads = [
        pltpu.make_async_copy(wi, wraw.at[0], load_w.at[0]),
        pltpu.make_async_copy(wo, wraw.at[1], load_w.at[1]),
    ]
    q_load = pltpu.make_async_copy(
        qin.at[:, pl.ds(pl.multiple_of(y * width, 128), width)], qbuf.at[y, c, x, z], load_q
    )
    q_load.start()
    w_loads[0].start()
    w_loads[1].start()
    order = [(dx % nx, i) for dx in range(1, nx + 1) for i in range(steps)]
    loads = []
    for n, (dx, i) in enumerate(order):
        first = pl.multiple_of(at(x, dx, nx) * part + i * chunk, 16)
        pair = (
            pltpu.make_async_copy(act.at[pl.ds(first, chunk), :], abuf.at[n], load_a.at[n]),
            pltpu.make_async_copy(og.at[pl.ds(first, chunk), :], gbuf.at[n], load_g.at[n]),
        )
        pair[0].start()
        pair[1].start()
        loads.append(pair)

    barrier = pltpu.get_barrier_semaphore()
    peers = [
        {"proj": at(x, dx, nx), "blk": at(z, dz, nz)}
        for dx in range(nx) for dz in range(nz) if dx or dz
    ]
    peers += [{"groups": at(y, dy, ny)} for dy in range(1, ny)]
    peers += [{"rep": at(c, dc, nc)} for dc in range(1, nc)]
    for peer in peers:
        pl.semaphore_signal(barrier, inc=1, device_id=peer, device_id_type=pl.DeviceIdType.MESH)

    lengths = counts[...].astype(F32)
    named = owners[...].astype(F32)
    row = lax.broadcasted_iota(jnp.int32, (docs, docs), 0)
    col = lax.broadcasted_iota(jnp.int32, (docs, docs), 1)
    starts = jnp.sum(jnp.where(col < row, lengths, 0.0), axis=1, keepdims=True)
    ends = jnp.sum(jnp.where(col <= row, lengths, 0.0), axis=1, keepdims=True)
    mine = jnp.sum(jnp.where(col == row, named, 0.0), axis=1, keepdims=True)
    rank = jnp.sum(
        jnp.where((col < row) & (named == mine), 1.0, 0.0), axis=1, keepdims=True
    )
    slot = (mine * CAP + rank).astype(jnp.int32)
    hit = slot == lax.broadcasted_iota(jnp.int32, (docs, columns), 1)
    col_start = jnp.sum(jnp.where(hit, starts, 0.0), axis=0, keepdims=True).astype(jnp.int32)
    col_end = jnp.sum(jnp.where(hit, ends, 0.0), axis=0, keepdims=True).astype(jnp.int32)

    for w in w_loads:
        w.wait()
    blank = jnp.zeros((wi.shape[0], ko), BF16)
    wpad[0] = jnp.concatenate([wraw[0], blank], axis=1)
    wpad[1] = jnp.concatenate([blank, wraw[1]], axis=1)
    q_load.wait()
    pl.semaphore_wait(barrier, len(peers))

    pending = []
    qa = {}
    qb = {}
    for dx in range(1, nx):
        qa[dx] = put(qbuf.at[y, c, x, z], qbuf.at[y, c, x, z], a_send.at[dx], a_recv.at[dx],
                     proj=at(x, dx, nx))
        qa[dx].start()

    def spread(j):
        from_x = at(x, nx - j, nx)
        for dz in range(1, nz):
            qb[j, dz] = put(qbuf.at[y, c, from_x, z], qbuf.at[y, c, from_x, z],
                            b_send.at[j, dz], b_recv.at[j, dz], blk=at(z, dz, nz))
            qb[j, dz].start()

    spread(0)

    def factors(n):
        loads[n][0].wait()
        loads[n][1].wait()
        return jnp.dot(abuf[n], wpad[0], preferred_element_type=F32) + jnp.dot(
            gbuf[n], wpad[1], preferred_element_type=F32
        )

    fx = {}
    for n, (dx, i) in enumerate(order):
        if dx == 0:
            break
        sbuf[dx - 1, i] = factors(n).astype(BF16)
        fx[dx, i] = put(sbuf.at[dx - 1, i], rbuf.at[dx - 1, i], fsend.at[dx - 1, i],
                        frecv.at[dx - 1, i], proj=at(x, dx, nx))
        fx[dx, i].start()
        if n == 0:
            for j in range(1, nx):
                qa[j].wait_recv()
                spread(j)

    yz = [
        put(qbuf.at[y, c], qbuf.at[y, c], c_send.at[dy], c_recv.at[dy], groups=at(y, dy, ny))
        for dy in range(1, ny)
    ]

    def to_cores(dy):
        from_y = at(y, ny - dy, ny)
        found = []
        for dc in range(1, nc):
            copy = put(qbuf.at[from_y, c], qbuf.at[from_y, c], d_send.at[dy, dc],
                       d_recv.at[dy, dc], rep=at(c, dc, nc))
            copy.start()
            found.append(copy)
        return found

    cores = []
    group = 8 * ko
    for i in range(steps):
        own = factors((nx - 1) * steps + i)
        if i == steps - 1:
            for copy in qb.values():
                copy.wait_recv()
            for copy in yz:
                copy.start()
            cores += to_cores(0)
        for dx in range(1, nx):
            fx[dx, i].wait_recv()
            own = own + rbuf[dx - 1, i].astype(F32)
        ft[...] = own.T
        position = x * part + i * chunk + lax.broadcasted_iota(jnp.int32, (chunk, columns), 0)
        member = jnp.where(
            (position >= col_start) & (position < col_end), 1.0, 0.0
        ).astype(BF16)

        def body(k, carry):
            out_t = ft[ki:ki + ko, :]
            in_t = ft[pl.ds(pl.multiple_of(k * 8, 8), 8), :]
            grads = jnp.concatenate(
                [(in_t[b:b + 1, :] * out_t).astype(BF16) for b in range(8)], axis=0
            )
            total = jnp.dot(grads, member, preferred_element_type=F32)
            rows = pl.ds(pl.multiple_of(k * group, group), group)
            if i > 0:
                total = total + dg[rows, :]
            if i < steps - 1:
                dg[rows, :] = total
            else:
                dgb[rows, :] = total.astype(BF16)
            return carry

        lax.fori_loop(0, ki // 8, body, 0)

    for dy in range(1, ny):
        yz[dy - 1].wait_recv()
        cores += to_cores(dy)
    for copy in cores:
        copy.wait_recv()

    total = None
    for xx in range(nx):
        for yy in range(ny):
            queries = jnp.concatenate(
                [qbuf[yy, cc, xx, zz] for cc in range(nc) for zz in range(nz)], axis=0
            )
            base = (xx * ny + yy) * width
            term = jnp.dot(queries, dgb[base:base + width, :], preferred_element_type=F32)
            total = term if total is None else total + term
    scores[...] = total

    per = nz // nx
    half = per * nc * qrows // 2
    low_lanes = lax.broadcasted_iota(jnp.int32, (half, 2 * CAP), 1) < CAP
    for xx in range(nx):
        starts_at = [
            (cc * nz + xx * per + zz) * qrows for zz in range(per) for cc in range(nc)
        ]
        for pair in range(nz // 2):
            lanes = slice(pair * 2 * CAP, (pair + 1) * 2 * CAP)
            block = jnp.concatenate([scores[s:s + qrows, lanes] for s in starts_at], axis=0)
            low, high = block[:half], block[half:]
            spack[2 * pair, xx] = jnp.where(low_lanes, low, pltpu.roll(high, CAP, 1))
            spack[2 * pair + 1, xx] = jnp.where(low_lanes, pltpu.roll(low, CAP, 1), high)
    sx = []
    for dx in range(nx):
        for dz in range(nz):
            if dx or dz:
                to_x, to_z = at(x, dx, nx), at(z, dz, nz)
                copy = put(spack.at[to_z, to_x], rpack.at[z, x], s_send.at[dx, dz],
                           s_recv.at[dx, dz], proj=to_x, blk=to_z)
                copy.start()
                sx.append(copy)
    rpack[z, x] = spack[z, x]
    for copy in sx:
        copy.wait_recv()
    for pair in range(nz // 2):
        lanes = slice(pair * 2 * CAP, (pair + 1) * 2 * CAP)
        left, right = rpack[2 * pair, 0], rpack[2 * pair + 1, 0]
        for xx in range(1, nx):
            left = left + rpack[2 * pair, xx]
            right = right + rpack[2 * pair + 1, xx]
        out[:half, lanes] = jnp.where(low_lanes, left, pltpu.roll(right, CAP, 1))
        out[half:, lanes] = jnp.where(low_lanes, pltpu.roll(left, CAP, 1), right)

    for copy in [*qa.values(), *qb.values(), *fx.values(), *yz, *cores, *sx]:
        copy.wait_send()


def per_device(sizes, activations, out_grads, in_proj, out_proj, precond_queries, counts, owners):
    ny, nz, nx, nc = sizes
    tokens, depth = activations.shape
    ki, ko = in_proj.shape[1], out_proj.shape[1]
    part = tokens // nx
    chunk = 384 if part % 384 == 0 else part
    steps = part // chunk
    count = nx * steps
    qrows, qcols = precond_queries.shape
    width = qcols // ny
    columns = nz * CAP
    feats = ki * ko
    queries = nz * nc * qrows
    rows = queries // nx
    dma = pltpu.SemaphoreType.DMA
    hbm = pl.BlockSpec(memory_space=pl.ANY)
    vmem = pl.BlockSpec(memory_space=pltpu.VMEM)
    others = max(nx - 1, 1)
    return pl.pallas_call(
        functools.partial(kernel, (*sizes, part, chunk)),
        out_shape=jax.ShapeDtypeStruct((rows, nz * CAP), F32),
        in_specs=[hbm] * 5 + [vmem] * 2,
        out_specs=vmem,
        scratch_shapes=[
            pltpu.VMEM((count, chunk, depth), BF16),
            pltpu.VMEM((count, chunk, depth), BF16),
            pltpu.VMEM((2, depth, ki), BF16),
            pltpu.VMEM((2, depth, ki + ko), BF16),
            pltpu.VMEM((ny, nc, nx, nz, qrows, width), BF16),
            pltpu.VMEM((others, steps, chunk, ki + ko), BF16),
            pltpu.VMEM((others, steps, chunk, ki + ko), BF16),
            pltpu.VMEM((feats, columns) if steps > 1 else (8, 128), F32),
            pltpu.VMEM((feats, columns), BF16),
            pltpu.VMEM((ki + ko, chunk), F32),
            pltpu.VMEM((queries, columns), F32),
            pltpu.VMEM((nz, nx, rows // 2, 2 * CAP), F32),
            pltpu.VMEM((nz, nx, rows // 2, 2 * CAP), F32),
            dma((count,)),
            dma((count,)),
            dma((2,)),
            dma,
            dma((others, steps)),
            dma((others, steps)),
            dma((nx,)),
            dma((nx,)),
            dma((nx, nz)),
            dma((nx, nz)),
            dma((ny,)),
            dma((ny,)),
            dma((ny, nc)),
            dma((ny, nc)),
            dma((nx, nz)),
            dma((nx, nz)),
        ],
        compiler_params=pltpu.CompilerParams(
            collective_id=0, has_side_effects=True, vmem_limit_bytes=56 * 1024 * 1024
        ),
        cost_estimate=pl.CostEstimate(
            flops=4 * tokens * depth * ki + 2 * part * feats * columns,
            bytes_accessed=4 * tokens * depth,
            transcendentals=0,
        ),
    )(activations, out_grads, in_proj, out_proj, precond_queries, counts, owners)


def solution(mesh):
    placed = (
        P(("groups", "blk", "rep"), "proj"),
        P(("groups", "blk", "rep"), "proj"),
        P("proj", None),
        P("proj", None),
        P(("blk", "rep"), "proj"),
        P(("groups", "blk", "rep"), None),
        P(("groups", "blk", "rep"), None),
    )
    sizes = tuple(mesh.shape[name] for name in ("groups", "blk", "proj", "rep"))
    return jax.shard_map(
        functools.partial(per_device, sizes),
        mesh=mesh,
        in_specs=placed,
        out_specs=P("proj", ("groups", "blk", "rep")),
        check_vma=False,
    )
```

```python
import functools

import jax
import jax.numpy as jnp
from jax import lax
from jax.experimental import pallas as pl
from jax.experimental.pallas import tpu as pltpu
from jax.sharding import PartitionSpec as P

CAP = 64
F32 = jnp.float32
BF16 = jnp.bfloat16


def kernel(sizes, act, og, wi, wo, qin, counts, owners, out, abuf, gbuf, wraw, wpad, qbuf, sbuf,
           rbuf, own, dg, dgb, ft, scores, spack, rpack, load_a, load_g, load_w, load_q, fsend,
           frecv, a_send, a_recv, b_send, b_recv, c_send, c_recv, d_send, d_recv, s_send, s_recv):
    ny, nz, nx, nc, part, chunks = sizes
    steps = len(chunks)
    x, y = lax.axis_index("proj"), lax.axis_index("groups")
    z, c = lax.axis_index("blk"), lax.axis_index("rep")
    ki, ko = wi.shape[0], wo.shape[0]
    width = qbuf.shape[-1]
    qrows = qin.shape[0]
    docs = counts.shape[1]
    columns = nz * CAP

    def put(src, dst, send, recv, **where):
        return pltpu.make_async_remote_copy(
            src_ref=src, dst_ref=dst, send_sem=send, recv_sem=recv,
            device_id=where, device_id_type=pl.DeviceIdType.MESH,
        )

    def at(index, step, n):
        return lax.rem(index + step, n)

    q_loads = [
        pltpu.make_async_copy(
            qin.at[:, yy * width:(yy + 1) * width], qbuf.at[yy, c, x, z], load_q.at[yy]
        )
        for yy in range(ny)
    ]
    w_loads = [
        pltpu.make_async_copy(wi, wraw.at[0], load_w.at[0]),
        pltpu.make_async_copy(wo, wraw.at[1], load_w.at[1]),
    ]
    for copy in [*w_loads, *q_loads]:
        copy.start()
    order = [(dx % nx, i) for dx in range(1, nx + 1) for i in range(steps)]
    loads = []
    for n, (dx, i) in enumerate(order):
        offset, size = chunks[i]
        first = pl.multiple_of(at(x, dx, nx) * part + offset, 16)
        rows = pl.ds(offset, size)
        pair = (
            pltpu.make_async_copy(
                act.at[pl.ds(first, size), :], abuf.at[dx, rows, :], load_a.at[n]
            ),
            pltpu.make_async_copy(
                og.at[pl.ds(first, size), :], gbuf.at[dx, rows, :], load_g.at[n]
            ),
        )
        pair[0].start()
        pair[1].start()
        loads.append(pair)

    barrier = pltpu.get_barrier_semaphore()
    peers = [
        {"proj": at(x, dx, nx), "blk": at(z, dz, nz)}
        for dx in range(nx) for dz in range(nz) if dx or dz
    ]
    peers += [{"groups": at(y, dy, ny)} for dy in range(1, ny)]
    peers += [{"rep": at(c, dc, nc)} for dc in range(1, nc)]
    for peer in peers:
        pl.semaphore_signal(barrier, inc=1, device_id=peer, device_id_type=pl.DeviceIdType.MESH)

    lengths = counts[...].astype(F32)
    named = owners[...].astype(F32)
    row = lax.broadcasted_iota(jnp.int32, (docs, docs), 0)
    col = lax.broadcasted_iota(jnp.int32, (docs, docs), 1)
    starts = jnp.sum(jnp.where(col < row, lengths, 0.0), axis=1, keepdims=True)
    ends = jnp.sum(jnp.where(col <= row, lengths, 0.0), axis=1, keepdims=True)
    mine = jnp.sum(jnp.where(col == row, named, 0.0), axis=1, keepdims=True)
    rank = jnp.sum(
        jnp.where((col < row) & (named == mine), 1.0, 0.0), axis=1, keepdims=True
    )
    slot = (mine * CAP + rank).astype(jnp.int32)
    hit = slot == lax.broadcasted_iota(jnp.int32, (docs, columns), 1)
    col_start = jnp.sum(jnp.where(hit, starts, 0.0), axis=0, keepdims=True).astype(jnp.int32)
    col_end = jnp.sum(jnp.where(hit, ends, 0.0), axis=0, keepdims=True).astype(jnp.int32)

    for w in w_loads:
        w.wait()
    blank = jnp.zeros((ki, wi.shape[1]), BF16)
    wpad[0] = jnp.concatenate([wraw[0], blank], axis=0).T
    wpad[1] = jnp.concatenate([blank, wraw[1]], axis=0).T

    def factors(n):
        dx, i = order[n]
        offset, size = chunks[i]
        loads[n][0].wait()
        loads[n][1].wait()
        rows = slice(offset, offset + size)
        return jnp.dot(abuf[dx, rows, :], wpad[0], preferred_element_type=F32) + jnp.dot(
            gbuf[dx, rows, :], wpad[1], preferred_element_type=F32
        )

    sent = []
    got = {}

    def piece(yy, j, dz):
        return qbuf.at[yy, c, at(x, nx - j, nx), at(z, nz - dz, nz)]

    def go(key, copy):
        copy.start()
        sent.append(copy)
        got[key] = copy

    def along_z(j):
        for dz in [1, *range(nz - 1, 1, -1)]:
            ref = piece(y, j, 0)
            go(("z", j, dz),
               put(ref, ref, b_send.at[j, dz], b_recv.at[j, dz], blk=at(z, dz, nz)))

    def along_y(j, dz):
        for dy in range(1, ny):
            ref = piece(y, j, dz)
            go(("y", dy, j, dz),
               put(ref, ref, c_send.at[dy, j, dz], c_recv.at[dy, j, dz], groups=at(y, dy, ny)))

    def to_core(dy, j, dz):
        for dc in range(1, nc):
            ref = piece(at(y, ny - dy, ny), j, dz)
            go(("c", dc, dy, j, dz),
               put(ref, ref, d_send.at[dy, dc, j, dz], d_recv.at[dy, dc, j, dz],
                   rep=at(c, dc, nc)))

    def from_z(dz):
        for j in range(nx):
            got["z", j, dz].wait_recv()
            along_y(j, dz)
            to_core(0, j, dz)

    def from_y(keys):
        for dy in range(1, ny):
            for j, dz in keys:
                got["y", dy, j, dz].wait_recv()
                to_core(dy, j, dz)

    def begin():
        for copy in q_loads:
            copy.wait()
        pl.semaphore_wait(barrier, len(peers))
        for dx in range(1, nx):
            ref = piece(y, 0, 0)
            go(("x", dx), put(ref, ref, a_send.at[dx], a_recv.at[dx], proj=at(x, dx, nx)))
        along_z(0)

    fx = {}
    if nx == 1:
        begin()
    for n, (dx, i) in enumerate(order):
        offset, size = chunks[i]
        rows = slice(offset, offset + size)
        if dx == 0:
            own[rows, :] = factors(n)
            if i == 0:
                for j in range(1, nx):
                    got["x", j].wait_recv()
                    along_z(j)
                    along_y(j, 0)
                    to_core(0, j, 0)
                for dy in range(ny):
                    to_core(dy, 0, 0)
            continue
        sbuf[dx - 1, rows, :] = factors(n).astype(BF16)
        if n == 0:
            begin()
        part_rows = pl.ds(offset, size)
        fx[dx, i] = put(sbuf.at[dx - 1, part_rows, :], rbuf.at[dx - 1, part_rows, :],
                        fsend.at[dx - 1, i], frecv.at[dx - 1, i], proj=at(x, dx, nx))
        fx[dx, i].start()

    near = [1, nz - 1] if nz > 2 else [1]
    far = [dz for dz in range(1, nz) if dz not in near]
    block = 32
    group = block * ko
    for i, (offset, size) in enumerate(chunks):
        rows = slice(offset, offset + size)
        if i == 0:
            from_z(near[0])
        if i == min(1, steps - 1):
            for dz in near[1:] + far:
                from_z(dz)
        if i == steps - 1:
            from_y([(j, 0) for j in range(1, nx)])
            for dz in near + far:
                from_y([(j, dz) for j in range(nx)])
        here = own[rows, :]
        for dx in range(1, nx):
            fx[dx, i].wait_recv()
            here = here + rbuf[dx - 1, rows, :].astype(F32)
        ft[:, :size] = here.T
        position = x * part + offset + lax.broadcasted_iota(jnp.int32, (size, columns), 0)
        member = jnp.where(
            (position >= col_start) & (position < col_end), 1.0, 0.0
        ).astype(BF16)

        def body(k, carry):
            out_t = ft[ki:ki + ko, :size]
            in_t = ft[pl.ds(pl.multiple_of(k * block, block), block), :size]
            grads = jnp.concatenate(
                [(in_t[b:b + 1, :] * out_t).astype(BF16) for b in range(block)], axis=0
            )
            total = jnp.dot(grads, member, preferred_element_type=F32)
            places = pl.ds(pl.multiple_of(k * group, group), group)
            if i > 0:
                total = total + dg[places, :]
            if i < steps - 1:
                dg[places, :] = total
            else:
                dgb[places, :] = total.astype(BF16)
            return carry

        lax.fori_loop(0, ki // block, body, 0)

    for key, copy in got.items():
        if key[0] == "c":
            copy.wait_recv()

    total = None
    for xx in range(nx):
        for yy in range(ny):
            queries = jnp.concatenate(
                [qbuf[yy, cc, xx, zz] for cc in range(nc) for zz in range(nz)], axis=0
            )
            base = (xx * ny + yy) * width
            term = jnp.dot(queries, dgb[base:base + width, :], preferred_element_type=F32)
            total = term if total is None else total + term
    scores[...] = total

    per = nz // nx
    half = per * nc * qrows // 2
    low_lanes = lax.broadcasted_iota(jnp.int32, (half, 2 * CAP), 1) < CAP
    for xx in range(nx):
        starts_at = [
            (cc * nz + xx * per + zz) * qrows for zz in range(per) for cc in range(nc)
        ]
        for pair in range(nz // 2):
            lanes = slice(pair * 2 * CAP, (pair + 1) * 2 * CAP)
            block = jnp.concatenate([scores[s:s + qrows, lanes] for s in starts_at], axis=0)
            low, high = block[:half], block[half:]
            spack[2 * pair, xx] = jnp.where(low_lanes, low, pltpu.roll(high, CAP, 1))
            spack[2 * pair + 1, xx] = jnp.where(low_lanes, pltpu.roll(low, CAP, 1), high)
    sx = []
    for dx in range(nx):
        for dz in range(nz):
            if dx or dz:
                to_x, to_z = at(x, dx, nx), at(z, dz, nz)
                copy = put(spack.at[to_z, to_x], rpack.at[z, x], s_send.at[dx, dz],
                           s_recv.at[dx, dz], proj=to_x, blk=to_z)
                copy.start()
                sx.append(copy)
    rpack[z, x] = spack[z, x]
    for copy in sx:
        copy.wait_recv()
    for pair in range(nz // 2):
        lanes = slice(pair * 2 * CAP, (pair + 1) * 2 * CAP)
        left, right = rpack[2 * pair, 0], rpack[2 * pair + 1, 0]
        for xx in range(1, nx):
            left = left + rpack[2 * pair, xx]
            right = right + rpack[2 * pair + 1, xx]
        out[:half, lanes] = jnp.where(low_lanes, left, pltpu.roll(right, CAP, 1))
        out[half:, lanes] = jnp.where(low_lanes, pltpu.roll(left, CAP, 1), right)

    for copy in [*sent, *fx.values(), *sx]:
        copy.wait_send()


def per_device(sizes, activations, out_grads, in_proj, out_proj, precond_queries, counts, owners):
    ny, nz, nx, nc = sizes
    tokens, depth = activations.shape
    ki, ko = in_proj.shape[1], out_proj.shape[1]
    part = tokens // nx
    chunks = tuple((first, min(512, part - first)) for first in range(0, part, 512))
    steps = len(chunks)
    count = nx * steps
    qrows, qcols = precond_queries.shape
    width = qcols // ny
    columns = nz * CAP
    feats = ki * ko
    queries = nz * nc * qrows
    rows = queries // nx
    dma = pltpu.SemaphoreType.DMA
    hbm = pl.BlockSpec(memory_space=pl.ANY)
    vmem = pl.BlockSpec(memory_space=pltpu.VMEM)
    others = max(nx - 1, 1)
    return pl.pallas_call(
        functools.partial(kernel, (*sizes, part, chunks)),
        out_shape=jax.ShapeDtypeStruct((rows, nz * CAP), F32),
        in_specs=[hbm] * 5 + [vmem] * 2,
        out_specs=vmem,
        scratch_shapes=[
            pltpu.VMEM((nx, part, depth), BF16),
            pltpu.VMEM((nx, part, depth), BF16),
            pltpu.VMEM((2, ki, depth), BF16),
            pltpu.VMEM((2, depth, ki + ko), BF16),
            pltpu.VMEM((ny, nc, nx, nz, qrows, width), BF16),
            pltpu.VMEM((others, part, ki + ko), BF16),
            pltpu.VMEM((others, part, ki + ko), BF16),
            pltpu.VMEM((part, ki + ko), F32),
            pltpu.VMEM((feats, columns) if steps > 1 else (8, 128), F32),
            pltpu.VMEM((feats, columns), BF16),
            pltpu.VMEM((ki + ko, chunks[0][1]), F32),
            pltpu.VMEM((queries, columns), F32),
            pltpu.VMEM((nz, nx, rows // 2, 2 * CAP), F32),
            pltpu.VMEM((nz, nx, rows // 2, 2 * CAP), F32),
            dma((count,)),
            dma((count,)),
            dma((2,)),
            dma((ny,)),
            dma((others, steps)),
            dma((others, steps)),
            dma((nx,)),
            dma((nx,)),
            dma((nx, nz)),
            dma((nx, nz)),
            dma((ny, nx, nz)),
            dma((ny, nx, nz)),
            dma((ny, nc, nx, nz)),
            dma((ny, nc, nx, nz)),
            dma((nx, nz)),
            dma((nx, nz)),
        ],
        compiler_params=pltpu.CompilerParams(
            collective_id=0, has_side_effects=True, vmem_limit_bytes=56 * 1024 * 1024
        ),
        cost_estimate=pl.CostEstimate(
            flops=4 * tokens * depth * ki + 2 * part * feats * columns,
            bytes_accessed=4 * tokens * depth,
            transcendentals=0,
        ),
    )(activations, out_grads, in_proj.T, out_proj.T, precond_queries, counts, owners)


def solution(mesh):
    placed = (
        P(("groups", "blk", "rep"), "proj"),
        P(("groups", "blk", "rep"), "proj"),
        P("proj", None),
        P("proj", None),
        P(("blk", "rep"), "proj"),
        P(("groups", "blk", "rep"), None),
        P(("groups", "blk", "rep"), None),
    )
    sizes = tuple(mesh.shape[name] for name in ("groups", "blk", "proj", "rep"))
    return jax.shard_map(
        functools.partial(per_device, sizes),
        mesh=mesh,
        in_specs=placed,
        out_specs=P("proj", ("groups", "blk", "rep")),
        check_vma=False,
    )
```

```python
import functools

import jax
import jax.numpy as jnp
from jax import lax
from jax.experimental import pallas as pl
from jax.experimental.pallas import tpu as pltpu
from jax.sharding import PartitionSpec as P

CAP = 64
CHUNK = 384
GROUP = 4
F32 = jnp.float32
BF16 = jnp.bfloat16


def kernel(sizes, act, og, wi, wo, qin, counts, owners, out, abuf, gbuf, wraw, wpad, qbuf, sbuf,
           rbuf, own, dgb, ft, scores, spack, rpack, load_a, load_g, load_w, load_q, fsend,
           frecv, a_send, a_recv, b_send, b_recv, c_send, c_recv, d_send, d_recv, s_send, s_recv):
    ny, nz, nx, nc, part, chunks = sizes
    steps = len(chunks)
    x, y = lax.axis_index("proj"), lax.axis_index("groups")
    z, c = lax.axis_index("blk"), lax.axis_index("rep")
    ki, ko = wi.shape[0], wo.shape[0]
    width = qbuf.shape[-1]
    qrows = qin.shape[0]
    docs = counts.shape[1]
    columns = nz * CAP

    def put(src, dst, send, recv, **where):
        return pltpu.make_async_remote_copy(
            src_ref=src, dst_ref=dst, send_sem=send, recv_sem=recv,
            device_id=where, device_id_type=pl.DeviceIdType.MESH,
        )

    def at(index, step, n):
        return lax.rem(index + step, n)

    q_loads = [
        pltpu.make_async_copy(
            qin.at[:, yy * width:(yy + 1) * width], qbuf.at[yy, c, x, z], load_q.at[yy]
        )
        for yy in range(ny)
    ]
    w_loads = [
        pltpu.make_async_copy(wi, wraw.at[0], load_w.at[0]),
        pltpu.make_async_copy(wo, wraw.at[1], load_w.at[1]),
    ]
    for copy in [*w_loads, *q_loads]:
        copy.start()
    order = [(dx % nx, i) for dx in range(1, nx + 1) for i in range(steps)]
    loads = []
    for n, (dx, i) in enumerate(order):
        offset, size = chunks[i]
        first = pl.multiple_of(at(x, dx, nx) * part + offset, 16)
        rows = pl.ds(offset, size)
        pair = (
            pltpu.make_async_copy(
                act.at[pl.ds(first, size), :], abuf.at[dx, rows, :], load_a.at[n]
            ),
            pltpu.make_async_copy(
                og.at[pl.ds(first, size), :], gbuf.at[dx, rows, :], load_g.at[n]
            ),
        )
        pair[0].start(priority=1)
        pair[1].start(priority=1)
        loads.append(pair)

    barrier = pltpu.get_barrier_semaphore()
    peers = [
        {"proj": at(x, dx, nx), "blk": at(z, dz, nz)}
        for dx in range(nx) for dz in range(nz) if dx or dz
    ]
    peers += [{"groups": at(y, dy, ny)} for dy in range(1, ny)]
    peers += [{"rep": at(c, dc, nc)} for dc in range(1, nc)]
    for peer in peers:
        pl.semaphore_signal(barrier, inc=1, device_id=peer, device_id_type=pl.DeviceIdType.MESH)

    lengths = counts[...].astype(F32)
    named = owners[...].astype(F32)
    row = lax.broadcasted_iota(jnp.int32, (docs, docs), 0)
    col = lax.broadcasted_iota(jnp.int32, (docs, docs), 1)
    starts = jnp.sum(jnp.where(col < row, lengths, 0.0), axis=1, keepdims=True)
    ends = jnp.sum(jnp.where(col <= row, lengths, 0.0), axis=1, keepdims=True)
    mine = jnp.sum(jnp.where(col == row, named, 0.0), axis=1, keepdims=True)
    rank = jnp.sum(
        jnp.where((col < row) & (named == mine), 1.0, 0.0), axis=1, keepdims=True
    )
    slot = (mine * CAP + rank).astype(jnp.int32)
    hit = slot == lax.broadcasted_iota(jnp.int32, (docs, columns), 1)
    col_start = jnp.sum(jnp.where(hit, starts, 0.0), axis=0, keepdims=True).astype(jnp.int32)
    col_end = jnp.sum(jnp.where(hit, ends, 0.0), axis=0, keepdims=True).astype(jnp.int32)

    for w in w_loads:
        w.wait()
    blank = jnp.zeros((ki, wi.shape[1]), BF16)
    wpad[0] = jnp.concatenate([wraw[0], blank], axis=0).T
    wpad[1] = jnp.concatenate([blank, wraw[1]], axis=0).T

    def factors(n):
        dx, i = order[n]
        offset, size = chunks[i]
        loads[n][0].wait()
        loads[n][1].wait()
        rows = slice(offset, offset + size)
        return jnp.dot(abuf[dx, rows, :], wpad[0], preferred_element_type=F32) + jnp.dot(
            gbuf[dx, rows, :], wpad[1], preferred_element_type=F32
        )

    sent = []
    got = {}

    def piece(yy, j, dz):
        return qbuf.at[yy, c, at(x, nx - j, nx), at(z, nz - dz, nz)]

    def go(key, copy):
        copy.start()
        sent.append(copy)
        got[key] = copy

    def along_z(j):
        for dz in [1, *range(nz - 1, 1, -1)]:
            ref = piece(y, j, 0)
            go(("z", j, dz),
               put(ref, ref, b_send.at[j, dz], b_recv.at[j, dz], blk=at(z, dz, nz)))

    def along_y(j, dz):
        for dy in range(1, ny):
            ref = piece(y, j, dz)
            go(("y", dy, j, dz),
               put(ref, ref, c_send.at[dy, j, dz], c_recv.at[dy, j, dz], groups=at(y, dy, ny)))

    def to_core(dy, j, dz):
        for dc in range(1, nc):
            ref = piece(at(y, ny - dy, ny), j, dz)
            go(("c", dc, dy, j, dz),
               put(ref, ref, d_send.at[dy, dc, j, dz], d_recv.at[dy, dc, j, dz],
                   rep=at(c, dc, nc)))

    def from_z(dz):
        for j in range(nx):
            got["z", j, dz].wait_recv()
            along_y(j, dz)
            to_core(0, j, dz)

    def from_y(keys):
        for dy in range(1, ny):
            for j, dz in keys:
                got["y", dy, j, dz].wait_recv()
                to_core(dy, j, dz)

    def begin():
        for copy in q_loads:
            copy.wait()
        pl.semaphore_wait(barrier, len(peers))
        for dx in range(1, nx):
            ref = piece(y, 0, 0)
            go(("x", dx), put(ref, ref, a_send.at[dx], a_recv.at[dx], proj=at(x, dx, nx)))
        along_z(0)

    fx = {}
    if nx == 1:
        begin()
    for n, (dx, i) in enumerate(order):
        offset, size = chunks[i]
        rows = slice(offset, offset + size)
        if dx == 0:
            own[rows, :] = factors(n)
            continue
        sbuf[dx - 1, rows, :] = factors(n).astype(BF16)
        if n == 0:
            begin()
        if n == len(order) - steps - 1:
            for j in range(1, nx):
                got["x", j].wait_recv()
                along_z(j)
                along_y(j, 0)
                to_core(0, j, 0)
            for dy in range(ny):
                to_core(dy, 0, 0)
            for to_x, k in order[:n + 1]:
                held = pl.ds(*chunks[k])
                fx[to_x, k] = put(
                    sbuf.at[to_x - 1, held, :], rbuf.at[to_x - 1, held, :],
                    fsend.at[to_x - 1, k], frecv.at[to_x - 1, k], proj=at(x, to_x, nx))
                fx[to_x, k].start()

    near = [1, nz - 1] if nz > 2 else [1]
    far = [dz for dz in range(1, nz) if dz not in near]
    from_z(near[0])
    for i, (offset, size) in enumerate(chunks):
        rows = slice(offset, offset + size)
        here = own[rows, :]
        for dx in range(1, nx):
            fx[dx, i].wait_recv()
            here = here + rbuf[dx - 1, rows, :].astype(F32)
        ft[:, rows] = here.T
        if i == 0:
            for dz in near[1:] + far:
                from_z(dz)
    from_y([(j, 0) for j in range(1, nx)])
    for dz in near:
        from_y([(j, dz) for j in range(nx)])
    position = x * part + lax.broadcasted_iota(jnp.int32, (part, columns), 0)
    member = jnp.where(
        (position >= col_start) & (position < col_end), 1.0, 0.0
    ).astype(BF16)
    for first in range(0, ki, GROUP):
        if first == ki // 2:
            for dz in far:
                from_y([(j, dz) for j in range(nx)])
        out_t = ft[ki:, :]
        grads = jnp.concatenate(
            [(ft[b:b + 1, :] * out_t).astype(BF16) for b in range(first, first + GROUP)], axis=0
        )
        dgb[first * ko:(first + GROUP) * ko, :] = jnp.dot(
            grads, member, preferred_element_type=F32
        ).astype(BF16)

    for key, copy in got.items():
        if key[0] == "c":
            copy.wait_recv()

    total = None
    for xx in range(nx):
        for yy in range(ny):
            queries = jnp.concatenate(
                [qbuf[yy, cc, xx, zz] for cc in range(nc) for zz in range(nz)], axis=0
            )
            base = (xx * ny + yy) * width
            term = jnp.dot(queries, dgb[base:base + width, :], preferred_element_type=F32)
            total = term if total is None else total + term
    scores[...] = total

    per = nz // nx
    half = per * nc * qrows // 2
    low_lanes = lax.broadcasted_iota(jnp.int32, (half, 2 * CAP), 1) < CAP
    for xx in range(nx):
        starts_at = [
            (cc * nz + xx * per + zz) * qrows for zz in range(per) for cc in range(nc)
        ]
        for pair in range(nz // 2):
            lanes = slice(pair * 2 * CAP, (pair + 1) * 2 * CAP)
            block = jnp.concatenate([scores[s:s + qrows, lanes] for s in starts_at], axis=0)
            low, high = block[:half], block[half:]
            spack[2 * pair, xx] = jnp.where(low_lanes, low, pltpu.roll(high, CAP, 1))
            spack[2 * pair + 1, xx] = jnp.where(low_lanes, pltpu.roll(low, CAP, 1), high)
    sx = []
    for dx in range(nx):
        for dz in range(nz):
            if dx or dz:
                to_x, to_z = at(x, dx, nx), at(z, dz, nz)
                copy = put(spack.at[to_z, to_x], rpack.at[z, x], s_send.at[dx, dz],
                           s_recv.at[dx, dz], proj=to_x, blk=to_z)
                copy.start()
                sx.append(copy)
    rpack[z, x] = spack[z, x]
    for copy in sx:
        copy.wait_recv()
    for pair in range(nz // 2):
        lanes = slice(pair * 2 * CAP, (pair + 1) * 2 * CAP)
        left, right = rpack[2 * pair, 0], rpack[2 * pair + 1, 0]
        for xx in range(1, nx):
            left = left + rpack[2 * pair, xx]
            right = right + rpack[2 * pair + 1, xx]
        out[:half, lanes] = jnp.where(low_lanes, left, pltpu.roll(right, CAP, 1))
        out[half:, lanes] = jnp.where(low_lanes, pltpu.roll(left, CAP, 1), right)

    for copy in [*sent, *fx.values(), *sx]:
        copy.wait_send()


def per_device(sizes, activations, out_grads, in_proj, out_proj, precond_queries, counts, owners):
    ny, nz, nx, nc = sizes
    tokens, depth = activations.shape
    ki, ko = in_proj.shape[1], out_proj.shape[1]
    part = tokens // nx
    chunks = tuple((first, min(CHUNK, part - first)) for first in range(0, part, CHUNK))
    steps = len(chunks)
    count = nx * steps
    qrows, qcols = precond_queries.shape
    width = qcols // ny
    columns = nz * CAP
    feats = ki * ko
    queries = nz * nc * qrows
    rows = queries // nx
    dma = pltpu.SemaphoreType.DMA
    hbm = pl.BlockSpec(memory_space=pl.ANY)
    vmem = pl.BlockSpec(memory_space=pltpu.VMEM)
    others = max(nx - 1, 1)
    return pl.pallas_call(
        functools.partial(kernel, (*sizes, part, chunks)),
        out_shape=jax.ShapeDtypeStruct((rows, nz * CAP), F32),
        in_specs=[hbm] * 5 + [vmem] * 2,
        out_specs=vmem,
        scratch_shapes=[
            pltpu.VMEM((nx, part, depth), BF16),
            pltpu.VMEM((nx, part, depth), BF16),
            pltpu.VMEM((2, ki, depth), BF16),
            pltpu.VMEM((2, depth, ki + ko), BF16),
            pltpu.VMEM((ny, nc, nx, nz, qrows, width), BF16),
            pltpu.VMEM((others, part, ki + ko), BF16),
            pltpu.VMEM((others, part, ki + ko), BF16),
            pltpu.VMEM((part, ki + ko), F32),
            pltpu.VMEM((feats, columns), BF16),
            pltpu.VMEM((ki + ko, part), F32),
            pltpu.VMEM((queries, columns), F32),
            pltpu.VMEM((nz, nx, rows // 2, 2 * CAP), F32),
            pltpu.VMEM((nz, nx, rows // 2, 2 * CAP), F32),
            dma((count,)),
            dma((count,)),
            dma((2,)),
            dma((ny,)),
            dma((others, steps)),
            dma((others, steps)),
            dma((nx,)),
            dma((nx,)),
            dma((nx, nz)),
            dma((nx, nz)),
            dma((ny, nx, nz)),
            dma((ny, nx, nz)),
            dma((ny, nc, nx, nz)),
            dma((ny, nc, nx, nz)),
            dma((nx, nz)),
            dma((nx, nz)),
        ],
        compiler_params=pltpu.CompilerParams(
            collective_id=0, has_side_effects=True, vmem_limit_bytes=56 * 1024 * 1024
        ),
        cost_estimate=pl.CostEstimate(
            flops=4 * tokens * depth * ki + 2 * part * feats * columns,
            bytes_accessed=4 * tokens * depth,
            transcendentals=0,
        ),
    )(activations, out_grads, in_proj.T, out_proj.T, precond_queries, counts, owners)


def solution(mesh):
    placed = (
        P(("groups", "blk", "rep"), "proj"),
        P(("groups", "blk", "rep"), "proj"),
        P("proj", None),
        P("proj", None),
        P(("blk", "rep"), "proj"),
        P(("groups", "blk", "rep"), None),
        P(("groups", "blk", "rep"), None),
    )
    sizes = tuple(mesh.shape[name] for name in ("groups", "blk", "proj", "rep"))
    return jax.shard_map(
        functools.partial(per_device, sizes),
        mesh=mesh,
        in_specs=placed,
        out_specs=P("proj", ("groups", "blk", "rep")),
        check_vma=False,
    )
```
